32 devices in a mesh: grp: 4 (over y, x), dev: 8 (over z, core).
Axes of the slice: x: 2, y: 2, z: 4, core: 2. Of those that a mesh axis runs over, the one named last changes fastest.
Arguments:
- noise_draws: bfloat16 [4096, 1024], P('dev', 'grp'), may hold values from -12 to 12
- latents: bfloat16 [2048, 1024], P(('grp', 'dev')), may hold values from -6 to 6
Outputs:
- targets: float32 [4096, 1024], P('dev', 'grp')
The draws below stay inside these ranges and needn't reach their ends.
All inputs are finite; a program needn't handle non-finite values.
Results may differ from the reference program's by a relative error of at most 0.0027.
Values may be sent and summed in bfloat16 or wider, within the bound.
A program may use at most 64 MiB of HBM per device.

```python
import math
import jax
import jax.numpy as jnp
from jax import lax

D = 1024
ITERS = 4
NOISE = 4096
DATA = 2048


def draw_noise_draws(key, part):
    first_key = jax.random.fold_in(key, 0)
    values = jax.random.normal(first_key, (NOISE, D), jnp.float32)
    return jnp.clip(values, -12.0, 12.0).astype(jnp.bfloat16)


def steps_of(key, shape, cuts, low, largest):
    def one(dim, shards_of):
        draws = jax.random.uniform(jax.random.fold_in(jax.random.fold_in(key, 6), dim), (shards_of,), jnp.float32, low / len(cuts), largest / len(cuts))
        return jnp.repeat(jnp.exp(draws), shape[dim] // shards_of).reshape((-1,) + (1,) * (len(shape) - dim - 1))

    factor_of = one(*cuts[0])
    for cut in cuts[1:]:
        factor_of = factor_of * one(*cut)
    return factor_of


def scatter_about(stream_key, extent, scale, limit, shards=(), held_as=jnp.bfloat16):
    factor_of = steps_of(stream_key, extent, shards, -0.22, 0.18) if shards else 1.0
    result = jax.random.normal(stream_key, extent, jnp.float32) * scale * factor_of
    return jnp.minimum(jnp.maximum(result, -limit), limit).astype(held_as)


def setup_inputs(seed: int = 0) -> dict:
    streams_of = jax.random.split(jax.random.key(seed), 3)
    noise_draws = draw_noise_draws(jax.random.fold_in(streams_of[2], 71), 0)
    latents = scatter_about(streams_of[1], (DATA, D), 1.0, 6.0, ((0, 32),))
    return dict(noise_draws=noise_draws, latents=latents)


def reference(noise_draws, latents):
    epsilon = 1.0 / math.sqrt(D)
    noise_sq = lax.optimization_barrier(jnp.sum(jnp.square(noise_draws.astype(jnp.float32)), axis=1))
    latent_sq = lax.optimization_barrier(jnp.sum(jnp.square(latents.astype(jnp.float32)), axis=1))
    cross_term = jnp.dot(noise_draws, latents.T, preferred_element_type=jnp.float32)
    cost_full = (noise_sq[:, None] + latent_sq[None, :] - 2.0 * cross_term) / D
    log_rows = -math.log(NOISE)
    log_cols = -math.log(DATA)
    column_dual = jnp.zeros((DATA,), jnp.float32)
    for sweep in range(ITERS):
        row_total = jax.nn.logsumexp((column_dual[None, :] - cost_full) / epsilon, axis=1)
        row_dual = epsilon * log_rows - epsilon * row_total
        column_total = jax.nn.logsumexp((row_dual[:, None] - cost_full) / epsilon, axis=0)
        column_dual = epsilon * log_cols - epsilon * column_total
    logits = (column_dual[None, :] - cost_full) / epsilon
    norm_total = jax.nn.logsumexp(logits, axis=1)
    weights = jnp.exp(logits - norm_total[:, None]).astype(jnp.bfloat16)
    return jnp.dot(weights, latents, preferred_element_type=jnp.float32)
```

```python
import functools
import math

import jax
import jax.numpy as jnp
from jax import lax
from jax.experimental import pallas as pl
from jax.experimental.pallas import tpu as pltpu
from jax.sharding import PartitionSpec as P

ITERS = 4
TILE = 128
LOG2E = 1.0 / math.log(2.0)
MESH = pl.DeviceIdType.MESH


def kernel(
    G, V, x_ref, y_ref, out_ref,
    xg, yg, cost, rowbuf, colbuf, dual, wbuf, sendbuf, recvbuf,
    xs, xr, ys, yr, hs, hr, rs, rr, cs, cr, os, orr,
):
    g = lax.axis_index("grp")
    d = lax.axis_index("dev")
    rows, feats = x_ref.shape
    segs, D = y_ref.shape
    cols = cost.shape[1]
    tiles = rows // TILE
    C = V // 2
    core = lax.rem(d, 2)
    sib = d + 1 - 2 * core

    def grp_peer(k):
        return lax.rem(g + k, G)

    def dev_peer(k):
        return lax.rem(d + k, V)

    barrier = pltpu.get_barrier_semaphore()
    for k in range(1, G):
        pl.semaphore_signal(barrier, inc=1, device_id={"grp": grp_peer(k)}, device_id_type=MESH)
    for k in range(1, V):
        pl.semaphore_signal(barrier, inc=1, device_id={"dev": dev_peer(k)}, device_id_type=MESH)
    pl.semaphore_wait(barrier, G - 1 + V - 1)

    def slot(ref, i):
        return ref.at[pl.ds(pl.multiple_of(i * segs, segs), segs), :]

    ycopies = []
    for k in range(1, C):
        c = pltpu.make_async_remote_copy(
            y_ref, slot(yg, d), ys.at[k], yr.at[k],
            device_id={"dev": dev_peer(2 * k)}, device_id_type=MESH)
        c.start()
        ycopies.append(c)
    xcopies = []
    for k in range(1, G):
        c = pltpu.make_async_remote_copy(
            x_ref, xg.at[k], xs.at[k], xr.at[k],
            device_id={"grp": grp_peer(k)}, device_id_type=MESH)
        c.start()
        xcopies.append(c)
    handed = [pltpu.make_async_remote_copy(
        y_ref, slot(yg, d), hs.at[0], hr.at[0], device_id={"dev": sib}, device_id_type=MESH)]
    handed[0].start()
    slot(yg, d)[...] = y_ref[...]
    xg[0] = x_ref[...]
    for k in range(1, C):
        ycopies[k - 1].wait_recv()
        src = lax.rem(d - 2 * k + V, V)
        c = pltpu.make_async_remote_copy(
            slot(yg, src), slot(yg, src), hs.at[k], hr.at[k],
            device_id={"dev": sib}, device_id_type=MESH)
        c.start()
        handed.append(c)
    for c in handed:
        c.wait_recv()

    r_i = lax.broadcasted_iota(jnp.int32, (TILE, TILE), 0)
    c_i = lax.broadcasted_iota(jnp.int32, (TILE, TILE), 1)
    eye = r_i == c_i

    def compact(v):
        return jnp.sum(jnp.where(eye, v, 0.0), axis=0, keepdims=True)

    def expand(v):
        return jnp.sum(jnp.where(eye, v, 0.0), axis=1, keepdims=True)

    unit = LOG2E * math.sqrt(D) / D
    for j in range(cols // TILE):
        yb = yg[pl.ds(j * TILE, TILE), :].astype(jnp.float32)
        dual[0:1, j * TILE:(j + 1) * TILE] = compact(jnp.sum(yb * yb, axis=1, keepdims=True))
    nsq = [jnp.zeros((TILE, 1), jnp.float32) for _ in range(tiles)]
    for k in range(G):
        if k:
            xcopies[k - 1].wait_recv()
        at = pl.multiple_of(lax.rem(g - k + G, G) * feats, feats)
        yk = yg[:, pl.ds(at, feats)]
        for t in range(tiles):
            xt = xg[k, t * TILE:(t + 1) * TILE, :]
            xf = xt.astype(jnp.float32)
            nsq[t] = nsq[t] + jnp.sum(xf * xf, axis=1, keepdims=True)
            part = lax.dot_general(
                xt, yk, (((1,), (1,)), ((), ())), preferred_element_type=jnp.float32)
            here = slice(t * TILE, (t + 1) * TILE)
            if k == 0:
                cost[here, :] = part
            elif k < G - 1:
                cost[here, :] += part
            else:
                cross = cost[here, :] + part
                cost[here, :] = (nsq[t] + dual[0:1, :] - 2.0 * cross) * unit
    for c in ycopies + xcopies + handed:
        c.wait_send()

    dual[...] = jnp.zeros_like(dual)
    log_rows = -math.log(rows * V) * LOG2E
    log_cols = -math.log(cols * G) * LOG2E

    def merge(parts):
        top = functools.reduce(jnp.maximum, parts)
        total = functools.reduce(lambda a, b: a + b, [jnp.exp2(p - top) for p in parts])
        return top + jnp.log(total) * LOG2E

    def row_lse(n):
        gd = dual[0:1, :]
        for t in range(tiles):
            v = gd - cost[t * TILE:(t + 1) * TILE, :]
            top = jnp.max(v, axis=1, keepdims=True)
            s = jnp.sum(jnp.exp2(v - top), axis=1, keepdims=True)
            rowbuf[n, 0, t:t + 1, :] = compact(top + jnp.log(s) * LOG2E)
        copies = []
        for k in range(1, G):
            c = pltpu.make_async_remote_copy(
                rowbuf.at[n, 0], rowbuf.at[n, k], rs.at[n, k], rr.at[n, k],
                device_id={"grp": grp_peer(k)}, device_id_type=MESH)
            c.start()
            copies.append(c)
        for c in copies:
            c.wait_recv()
        total = merge([rowbuf[n, k] for k in range(G)])
        for c in copies:
            c.wait_send()
        return total

    def sweep(n, carry):
        rd = log_rows - row_lse(n)
        fs = [expand(rd[t:t + 1, :]) for t in range(tiles)]
        tops = [jnp.max(fs[t] - cost[t * TILE:(t + 1) * TILE, :], axis=0, keepdims=True)
                for t in range(tiles)]
        top = functools.reduce(jnp.maximum, tops)
        s = functools.reduce(lambda a, b: a + b, [
            jnp.sum(jnp.exp2(fs[t] - cost[t * TILE:(t + 1) * TILE, :] - top), axis=0, keepdims=True)
            for t in range(tiles)])
        colbuf[n, 0] = top + jnp.log(s) * LOG2E
        copies = []
        for k in range(1, V):
            c = pltpu.make_async_remote_copy(
                colbuf.at[n, 0], colbuf.at[n, k], cs.at[n, k], cr.at[n, k],
                device_id={"dev": dev_peer(k)}, device_id_type=MESH)
            c.start()
            copies.append(c)
        for c in copies:
            c.wait_recv()
        dual[...] = log_cols - merge([colbuf[n, k] for k in range(V)])
        for c in copies:
            c.wait_send()
        return carry

    lax.fori_loop(0, ITERS, sweep, 0)
    total = row_lse(ITERS)
    gd = dual[0:1, :]
    for t in range(tiles):
        here = slice(t * TILE, (t + 1) * TILE)
        wbuf[here, :] = jnp.exp2(gd - cost[here, :] - expand(total[t:t + 1, :])).astype(jnp.bfloat16)

    def product(p):
        at = pl.multiple_of(p * feats, feats)
        return jnp.dot(wbuf[...], yg[:, pl.ds(at, feats)], preferred_element_type=jnp.float32)

    ocopies = []
    for k in range(1, G):
        sendbuf[k - 1] = product(grp_peer(k)).astype(jnp.bfloat16)
        c = pltpu.make_async_remote_copy(
            sendbuf.at[k - 1], recvbuf.at[k - 1], os.at[k], orr.at[k],
            device_id={"grp": grp_peer(k)}, device_id_type=MESH)
        c.start()
        ocopies.append(c)
    acc = product(g)
    for k in range(1, G):
        ocopies[k - 1].wait_recv()
        acc = acc + recvbuf[k - 1].astype(jnp.float32)
    out_ref[...] = acc
    for c in ocopies:
        c.wait_send()


def solution(mesh):
    G, V = mesh.shape["grp"], mesh.shape["dev"]

    def local(x, y):
        rows, feats = x.shape
        segs, D = y.shape
        cols = segs * V
        dma = pltpu.SemaphoreType.DMA
        f32, bf16 = jnp.float32, jnp.bfloat16
        return pl.pallas_call(
            functools.partial(kernel, G, V),
            out_shape=jax.ShapeDtypeStruct((rows, feats), f32),
            in_specs=[pl.BlockSpec(memory_space=pltpu.VMEM)] * 2,
            out_specs=pl.BlockSpec(memory_space=pltpu.VMEM),
            scratch_shapes=[
                pltpu.VMEM((G, rows, feats), bf16),
                pltpu.VMEM((cols, D), bf16),
                pltpu.VMEM((rows, cols), f32),
                pltpu.VMEM((ITERS + 1, G, rows // TILE, TILE), f32),
                pltpu.VMEM((ITERS, V, 1, cols), f32),
                pltpu.VMEM((1, cols), f32),
                pltpu.VMEM((rows, cols), bf16),
                pltpu.VMEM((G - 1, rows, feats), bf16),
                pltpu.VMEM((G - 1, rows, feats), bf16),
                dma((G,)), dma((G,)),
                dma((V // 2,)), dma((V // 2,)),
                dma((V // 2,)), dma((V // 2,)),
                dma((ITERS + 1, G)), dma((ITERS + 1, G)),
                dma((ITERS, V)), dma((ITERS, V)),
                dma((G,)), dma((G,)),
            ],
            compiler_params=pltpu.CompilerParams(
                collective_id=0, has_side_effects=True, vmem_limit_bytes=48 * 2**20),
        )(x, y)

    placed = (P("dev", "grp"), P(("grp", "dev"), None))
    return jax.shard_map(
        local, mesh=mesh, in_specs=placed, out_specs=P("dev", "grp"), check_vma=False)
```

```python
import functools
import math

import jax
import jax.numpy as jnp
from jax import lax
from jax.experimental import pallas as pl
from jax.experimental.pallas import tpu as pltpu
from jax.sharding import PartitionSpec as P

ITERS = 4
TILE = 128
LOG2E = 1.0 / math.log(2.0)
MESH = pl.DeviceIdType.MESH


def peer(i, k, n):
    if n & (n - 1):
        return lax.rem(i + k, n)
    j, b = i, 1
    while b < n:
        if k & b:
            j = j + b - 2 * b * lax.rem(i // b, 2)
        b *= 2
    return j


def source(i, k, n):
    return lax.rem(i - k + n, n) if n & (n - 1) else peer(i, k, n)


def wait_all(ref, sem):
    pltpu.make_async_copy(ref, ref, sem).wait()


def kernel(
    G, V, x_ref, y_ref, out_ref,
    xg, yall, cost, rowbuf, colbuf, gbuf, dual, segsq, wbuf, sendbuf, recvbuf,
    xs, xr, ys, yr, hs, hr, rs, rr, cs, cr, os, orr, ins, gs, gr, bs, br, ks, kr,
):
    g = lax.axis_index("grp")
    d = lax.axis_index("dev")
    yg = yall.at[0]
    rows, feats = x_ref.shape
    segs, D = y_ref.shape
    cols = cost.shape[1]
    part = rows // G
    piece = cols // (2 * ITERS)
    tiles = rows // TILE
    C = V // 2
    core = lax.rem(d, 2)
    chip = d // 2
    sib = d + 1 - 2 * core

    def slot(ref, i):
        return ref.at[pl.ds(pl.multiple_of(i * segs, segs), segs), :]

    mine = [pltpu.make_async_copy(y_ref, slot(yg, d), ins.at[0]),
            pltpu.make_async_copy(x_ref, xg.at[0], ins.at[1])]
    for c in mine:
        c.start()

    def grp_peer(k):
        return peer(g, k, G)

    def dev_peer(k):
        return peer(d, k, V)

    barrier = pltpu.get_barrier_semaphore()
    for k in range(1, G):
        pl.semaphore_signal(barrier, inc=1, device_id={"grp": grp_peer(k)}, device_id_type=MESH)
    for k in range(1, V):
        pl.semaphore_signal(barrier, inc=1, device_id={"dev": dev_peer(k)}, device_id_type=MESH)
    pl.semaphore_wait(barrier, G - 1 + V - 1)

    for c in mine:
        c.wait()

    ycopies = {}
    for k in range(1, C):
        ycopies[k] = pltpu.make_async_remote_copy(
            slot(yg, d), slot(yg, d), ys.at[k], yr.at[k],
            device_id={"dev": 2 * peer(chip, k, C) + core}, device_id_type=MESH)
        ycopies[k].start()
    xcopies = {}
    for k in range(1, G):
        xcopies[k] = pltpu.make_async_remote_copy(
            xg.at[0], xg.at[k], xs.at[k], xr.at[k],
            device_id={"grp": grp_peer(k)}, device_id_type=MESH)
        xcopies[k].start()
    handed = []
    for k in range(C):
        if k:
            ycopies[k].wait_recv()
        src = 2 * source(chip, k, C) + core if k else d
        c = pltpu.make_async_remote_copy(
            slot(yg, src), slot(yg, src), hs.at[k], hr.at[k],
            device_id={"dev": sib}, device_id_type=MESH)
        c.start()
        handed.append(c)
    for c in handed:
        c.wait_recv()

    r_i = lax.broadcasted_iota(jnp.int32, (TILE, TILE), 0)
    c_i = lax.broadcasted_iota(jnp.int32, (TILE, TILE), 1)
    eye = r_i == c_i

    def compact(v):
        return jnp.sum(jnp.where(eye, v, 0.0), axis=0, keepdims=True)

    def expand(v):
        return jnp.sum(jnp.where(eye, v, 0.0), axis=1, keepdims=True)

    unit = LOG2E * math.sqrt(D) / D
    for j in range(cols // TILE):
        yb = yg[pl.ds(j * TILE, TILE), :].astype(jnp.float32)
        dual[0:1, j * TILE:(j + 1) * TILE] = compact(jnp.sum(yb * yb, axis=1, keepdims=True))
    nsq = [jnp.zeros((TILE, 1), jnp.float32) for _ in range(tiles)]
    for k in range(G):
        if k:
            xcopies[k].wait_recv()
        at = pl.multiple_of((source(g, k, G) if k else g) * feats, feats)
        yk = yg[:, pl.ds(at, feats)]
        for t in range(tiles):
            xt = xg[k, t * TILE:(t + 1) * TILE, :]
            xf = xt.astype(jnp.float32)
            nsq[t] = nsq[t] + jnp.sum(xf * xf, axis=1, keepdims=True)
            prod = lax.dot_general(
                xt, yk, (((1,), (1,)), ((), ())), preferred_element_type=jnp.float32)
            here = slice(t * TILE, (t + 1) * TILE)
            if k == 0:
                cost[here, :] = prod
            elif k < G - 1:
                cost[here, :] += prod
            else:
                cross = cost[here, :] + prod
                cost[here, :] = (nsq[t] + dual[0:1, :] - 2.0 * cross) * unit
    for c in [*ycopies.values(), *xcopies.values(), *handed]:
        c.wait_send()

    segsq[...] = dual[...]
    dual[...] = jnp.zeros_like(dual)
    log_rows = -math.log(rows * V) * LOG2E
    log_cols = -math.log(cols * G) * LOG2E

    def merge(parts):
        top = functools.reduce(jnp.maximum, parts)
        total = functools.reduce(lambda a, b: a + b, [jnp.exp2(p - top) for p in parts])
        return top + jnp.log(total) * LOG2E

    def row_lse(n):
        gd = dual[0:1, :]
        for t in range(tiles):
            v = gd - cost[t * TILE:(t + 1) * TILE, :]
            top = jnp.max(v, axis=1, keepdims=True)
            s = jnp.sum(jnp.exp2(v - top), axis=1, keepdims=True)
            rowbuf[n, 0, t:t + 1, :] = compact(top + jnp.log(s) * LOG2E)
        for k in range(1, G):
            pltpu.make_async_remote_copy(
                rowbuf.at[n, 0], rowbuf.at[n, k], rs.at[n], rr.at[n],
                device_id={"grp": grp_peer(k)}, device_id_type=MESH).start()
        others = rowbuf.at[n, pl.ds(1, G - 1)]
        wait_all(others, rr.at[n])
        return merge([rowbuf[n, k] for k in range(G)])

    def span(k, n, c):
        at = pl.multiple_of(c * (cols // 2) + n * piece, piece)
        return yall.at[k, pl.ds(at, piece), :]

    def background(k, n):
        return pltpu.make_async_remote_copy(
            span(0, n, core), span(k, n, core), bs.at[n, k], br.at[n, k],
            device_id={"grp": grp_peer(k)}, device_id_type=MESH)

    def hand(k, n):
        return pltpu.make_async_remote_copy(
            span(k, n, core), span(k, n, core), ks.at[n, k], kr.at[n, k],
            device_id={"dev": sib}, device_id_type=MESH)

    def hand_on(n):
        for k in range(1, G):
            background(k, n).wait_recv()
            hand(k, n).start()

    def sweep(n, carry):
        rd = log_rows - row_lse(n)
        for k in range(1, G):
            background(k, n).start()

        @pl.when(n > 0)
        def _():
            hand_on(n - 1)

        fs = [expand(rd[t:t + 1, :]) for t in range(tiles)]
        tops = [jnp.max(fs[t] - cost[t * TILE:(t + 1) * TILE, :], axis=0, keepdims=True)
                for t in range(tiles)]
        top = functools.reduce(jnp.maximum, tops)
        s = functools.reduce(lambda a, b: a + b, [
            jnp.sum(jnp.exp2(fs[t] - cost[t * TILE:(t + 1) * TILE, :] - top), axis=0, keepdims=True)
            for t in range(tiles)])
        low = top + jnp.log(s) * LOG2E
        for j in range(cols // TILE):
            colbuf[n, 0, j:j + 1, :] = low[:, j * TILE:(j + 1) * TILE]
        for k in range(1, V):
            pltpu.make_async_remote_copy(
                colbuf.at[n, 0], colbuf.at[n, k], cs.at[n], cr.at[n],
                device_id={"dev": dev_peer(k)}, device_id_type=MESH).start()
        others = colbuf.at[n, pl.ds(1, V - 1)]
        wait_all(others, cr.at[n])
        cd = log_cols - merge([colbuf[n, k] for k in range(V)])
        for j in range(cols // TILE):
            dual[0:1, j * TILE:(j + 1) * TILE] = cd[j:j + 1, :]
        return carry

    lax.fori_loop(0, ITERS, sweep, 0)
    shift = dual[0:1, :] - segsq[0:1, :] * unit
    for j in range(cols // TILE):
        gbuf[0, j:j + 1, :] = shift[:, j * TILE:(j + 1) * TILE]
    for k in range(1, G):
        pltpu.make_async_remote_copy(
            gbuf.at[0], gbuf.at[k], gs.at[0], gr.at[0],
            device_id={"grp": grp_peer(k)}, device_id_type=MESH).start()
    hand_on(ITERS - 1)

    first = pl.multiple_of(g * part, part)
    sq = jnp.zeros((part, 1), jnp.float32)
    for k in range(G):
        xf = xg[k, pl.ds(first, part), :].astype(jnp.float32)
        sq = sq + jnp.sum(xf * xf, axis=1, keepdims=True)
    for b in range(G):
        if b:
            for n in range(ITERS):
                hand(b, n).wait_recv()
        for k in range(G):
            at = pl.multiple_of((source(g, k, G) if k else g) * feats, feats)
            prod = lax.dot_general(
                xg[k, pl.ds(first, part), :], yall[b, :, pl.ds(at, feats)],
                (((1,), (1,)), ((), ())), preferred_element_type=jnp.float32)
            cross = prod if k == 0 else cross + prod
        cost[b * part:(b + 1) * part, :] = (sq - 2.0 * cross) * unit
    others = gbuf.at[pl.ds(1, G - 1)]
    wait_all(others, gs.at[0])
    wait_all(others, gr.at[0])
    tops = []
    for b in range(G):
        block = slice(b * part, (b + 1) * part)
        for j in range(cols // TILE):
            dual[0:1, j * TILE:(j + 1) * TILE] = gbuf[b, j:j + 1, :]
        logits = dual[0:1, :] - cost[block, :]
        cost[block, :] = logits
        tops.append(jnp.max(logits, axis=1, keepdims=True))
    top = functools.reduce(jnp.maximum, tops)
    s = functools.reduce(lambda a, b: a + b, [
        jnp.sum(jnp.exp2(cost[b * part:(b + 1) * part, :] - top), axis=1, keepdims=True)
        for b in range(G)])
    total = top + jnp.log(s) * LOG2E
    for b in range(G):
        wbuf[b] = jnp.exp2(cost[b * part:(b + 1) * part, :] - total).astype(jnp.bfloat16)

    def product(p):
        at = pl.multiple_of(p * feats, feats)
        acc = None
        for b in range(G):
            term = jnp.dot(wbuf[b], yall[b, :, pl.ds(at, feats)],
                           preferred_element_type=jnp.float32)
            acc = term if acc is None else acc + term
        return acc

    ocopies = {}
    for k in range(G - 1, 0, -1):
        sendbuf[k - 1] = product(grp_peer(k)).astype(jnp.bfloat16)
        ocopies[k] = pltpu.make_async_remote_copy(
            sendbuf.at[k - 1], recvbuf.at[k - 1], os.at[k], orr.at[k],
            device_id={"grp": grp_peer(k)}, device_id_type=MESH)
        ocopies[k].start()
    out_ref[pl.ds(first, part), :] = product(g)
    for k in range(1, G):
        ocopies[k].wait_recv()
        at = pl.multiple_of(source(g, k, G) * part, part)
        out_ref[pl.ds(at, part), :] = recvbuf[k - 1].astype(jnp.float32)
    for c in ocopies.values():
        c.wait_send()

    def drain(n, carry):
        wait_all(colbuf.at[n, pl.ds(1, V - 1)], cs.at[n])
        wait_all(rowbuf.at[n, pl.ds(1, G - 1)], rs.at[n])
        for k in range(1, G):
            background(k, n).wait_send()
            hand(k, n).wait_send()
        return carry

    lax.fori_loop(0, ITERS, drain, 0)


def solution(mesh):
    G, V = mesh.shape["grp"], mesh.shape["dev"]

    def local(x, y):
        rows, feats = x.shape
        segs, D = y.shape
        cols = segs * V
        dma = pltpu.SemaphoreType.DMA
        f32, bf16 = jnp.float32, jnp.bfloat16
        return pl.pallas_call(
            functools.partial(kernel, G, V),
            out_shape=jax.ShapeDtypeStruct((rows, feats), f32),
            in_specs=[pl.BlockSpec(memory_space=pltpu.HBM)] * 2,
            out_specs=pl.BlockSpec(memory_space=pltpu.VMEM),
            scratch_shapes=[
                pltpu.VMEM((G, rows, feats), bf16),
                pltpu.VMEM((G, cols, D), bf16),
                pltpu.VMEM((rows, cols), f32),
                pltpu.VMEM((ITERS, G, rows // TILE, TILE), f32),
                pltpu.VMEM((ITERS, V, cols // TILE, TILE), f32),
                pltpu.VMEM((G, cols // TILE, TILE), f32),
                pltpu.VMEM((1, cols), f32),
                pltpu.VMEM((1, cols), f32),
                pltpu.VMEM((G, rows // G, cols), bf16),
                pltpu.VMEM((G - 1, rows // G, feats), bf16),
                pltpu.VMEM((G - 1, rows // G, feats), bf16),
                dma((G,)), dma((G,)),
                dma((V // 2,)), dma((V // 2,)),
                dma((V // 2,)), dma((V // 2,)),
                dma((ITERS,)), dma((ITERS,)),
                dma((ITERS,)), dma((ITERS,)),
                dma((G,)), dma((G,)),
                dma((2,)), dma((1,)), dma((1,)),
                dma((ITERS, G)), dma((ITERS, G)),
                dma((ITERS, G)), dma((ITERS, G)),
            ],
            compiler_params=pltpu.CompilerParams(
                collective_id=0, has_side_effects=True, vmem_limit_bytes=56 * 2**20),
        )(x, y)

    placed = (P("dev", "grp"), P(("grp", "dev"), None))
    return jax.shard_map(
        local, mesh=mesh, in_specs=placed, out_specs=P("dev", "grp"), check_vma=False)
```

```python
import functools
import math

import jax
import jax.numpy as jnp
from jax import lax
from jax.experimental import pallas as pl
from jax.experimental.pallas import tpu as pltpu
from jax.sharding import PartitionSpec as P

ITERS = 4
TILE = 128
CUTS = 4
LOG2E = 1.0 / math.log(2.0)
MESH = pl.DeviceIdType.MESH


def peer(i, k, n):
    if n & (n - 1):
        return lax.rem(i + k, n)
    j, b = i, 1
    while b < n:
        if k & b:
            j = j + b - 2 * b * lax.rem(i // b, 2)
        b *= 2
    return j


def source(i, k, n):
    return lax.rem(i - k + n, n) if n & (n - 1) else peer(i, k, n)


def wait_all(ref, sem):
    pltpu.make_async_copy(ref, ref, sem).wait()


def kernel(
    G, V, x_ref, y_ref, out_ref,
    xg, yall, cost, rowbuf, colbuf, gbuf, dual, segsq, wbuf, sendbuf, recvbuf,
    xs, xr, ys, yr, hs, hr, rs, rr, cs, cr, os, orr, ins, gs, gr, bs, br, ks, kr,
):
    g = lax.axis_index("grp")
    d = lax.axis_index("dev")
    yg = yall.at[0]
    rows, feats = x_ref.shape
    segs, D = y_ref.shape
    cols = cost.shape[1]
    part = rows // G
    piece = cols // (2 * ITERS)
    tiles = rows // TILE
    C = V // 2
    core = lax.rem(d, 2)
    chip = d // 2
    sib = d + 1 - 2 * core

    def slot(ref, i):
        return ref.at[pl.ds(pl.multiple_of(i * segs, segs), segs), :]

    mine = [pltpu.make_async_copy(y_ref, slot(yg, d), ins.at[0]),
            pltpu.make_async_copy(x_ref, xg.at[0], ins.at[1])]
    for c in mine:
        c.start()

    def grp_peer(k):
        return peer(g, k, G)

    def dev_peer(k):
        return peer(d, k, V)

    barrier = pltpu.get_barrier_semaphore()
    for k in range(1, G):
        pl.semaphore_signal(barrier, inc=1, device_id={"grp": grp_peer(k)}, device_id_type=MESH)
    for k in range(1, V):
        pl.semaphore_signal(barrier, inc=1, device_id={"dev": dev_peer(k)}, device_id_type=MESH)
    pl.semaphore_wait(barrier, G - 1 + V - 1)

    for c in mine:
        c.wait()

    def half(i, h):
        at = pl.multiple_of((2 * i + core) * segs + h * (segs // CUTS), segs // CUTS)
        return yg.at[pl.ds(at, segs // CUTS), :]

    def hop(way, s, h):
        block = half(chip - s * way, h)
        return pltpu.make_async_remote_copy(
            block, block, ys.at[(1 - way) // 2, s, h], yr.at[(1 - way) // 2, s, h],
            device_id={"dev": d + 2 * way}, device_id_type=MESH)

    def hand_half(way, s, h):
        block = half(chip - (s + 1) * way, h)
        return pltpu.make_async_remote_copy(
            block, block, hs.at[(1 - way) // 2, s, h], hr.at[(1 - way) // 2, s, h],
            device_id={"dev": sib}, device_id_type=MESH)

    def ahead(way, n):
        return chip + n < C if way > 0 else chip - n >= 0

    for h in range(CUTS):
        for way in (1, -1):
            @pl.when(ahead(way, 1))
            def _():
                hop(way, 0, h).start()

    relayed = G == 4
    step = rows // 2

    def noise(k, h, at=0, to=None):
        here = pl.ds(h * step, step)
        return pltpu.make_async_remote_copy(
            xg.at[at, here, :], xg.at[k, here, :], xs.at[k, h], xr.at[k, h],
            device_id={"grp": grp_peer(to or k)}, device_id_type=MESH)

    if relayed:
        for h in range(2):
            noise(1, h).start()
            noise(2, 1 - h).start()
    else:
        for k in range(1, G):
            for h in range(2):
                noise(k, h).start()
    own = pltpu.make_async_remote_copy(
        slot(yg, d), slot(yg, d), os.at[0], orr.at[0],
        device_id={"dev": sib}, device_id_type=MESH)
    own.start()

    def relay():
        noise(1, 0).wait_recv()
        noise(3, 0, 1, 2).start()
        noise(2, 1).wait_recv()
        noise(3, 1, 2, 1).start()

    for s in range(C - 1):
        for h in range(CUTS):
            for way in (1, -1):
                @pl.when(ahead(-way, s + 1))
                def _():
                    wait_all(half(chip - (s + 1) * way, h), yr.at[(1 - way) // 2, s, h])

                    @pl.when(ahead(way, 1))
                    def _():
                        if s + 1 < C - 1:
                            hop(way, s + 1, h).start()
                    hand_half(way, s, h).start()
        if s == 0 and relayed:
            relay()

    own.wait_recv()
    for s in range(C - 1):
        for h in range(CUTS):
            for way in (1, -1):
                @pl.when(ahead(-way, s + 1))
                def _():
                    hand_half(way, s, h).wait_recv()

    r_i = lax.broadcasted_iota(jnp.int32, (TILE, TILE), 0)
    c_i = lax.broadcasted_iota(jnp.int32, (TILE, TILE), 1)
    eye = r_i == c_i

    def compact(v):
        return jnp.sum(jnp.where(eye, v, 0.0), axis=0, keepdims=True)

    def expand(v):
        return jnp.sum(jnp.where(eye, v, 0.0), axis=1, keepdims=True)

    unit = LOG2E * math.sqrt(D) / D
    for j in range(cols // TILE):
        yb = yg[pl.ds(j * TILE, TILE), :].astype(jnp.float32)
        dual[0:1, j * TILE:(j + 1) * TILE] = compact(jnp.sum(yb * yb, axis=1, keepdims=True))
    nsq = [jnp.zeros((TILE, 1), jnp.float32) for _ in range(tiles)]
    for k in range(G):
        if k:
            for h in range(2):
                if not (relayed and k < 3 and h == k - 1):
                    noise(k, h).wait_recv()
        at = pl.multiple_of((source(g, k, G) if k else g) * feats, feats)
        yk = yg[:, pl.ds(at, feats)]
        for t in range(tiles):
            xt = xg[k, t * TILE:(t + 1) * TILE, :]
            xf = xt.astype(jnp.float32)
            nsq[t] = nsq[t] + jnp.sum(xf * xf, axis=1, keepdims=True)
            prod = lax.dot_general(
                xt, yk, (((1,), (1,)), ((), ())), preferred_element_type=jnp.float32)
            here = slice(t * TILE, (t + 1) * TILE)
            if k == 0:
                cost[here, :] = prod
            elif k < G - 1:
                cost[here, :] += prod
            else:
                cross = cost[here, :] + prod
                cost[here, :] = (nsq[t] + dual[0:1, :] - 2.0 * cross) * unit
    segsq[...] = dual[...]
    dual[...] = jnp.zeros_like(dual)
    log_rows = -math.log(rows * V) * LOG2E
    log_cols = -math.log(cols * G) * LOG2E

    def merge(parts):
        top = functools.reduce(jnp.maximum, parts)
        total = functools.reduce(lambda a, b: a + b, [jnp.exp2(p - top) for p in parts])
        return top + jnp.log(total) * LOG2E

    def row_lse(n):
        gd = dual[0:1, :]
        for t in range(tiles):
            v = gd - cost[t * TILE:(t + 1) * TILE, :]
            top = jnp.max(v, axis=1, keepdims=True)
            s = jnp.sum(jnp.exp2(v - top), axis=1, keepdims=True)
            rowbuf[n, 0, t:t + 1, :] = compact(top + jnp.log(s) * LOG2E)
        for k in range(1, G):
            pltpu.make_async_remote_copy(
                rowbuf.at[n, 0], rowbuf.at[n, k], rs.at[n], rr.at[n],
                device_id={"grp": grp_peer(k)}, device_id_type=MESH).start()
        others = rowbuf.at[n, pl.ds(1, G - 1)]
        wait_all(others, rr.at[n])
        return merge([rowbuf[n, k] for k in range(G)])

    def span(k, n, c):
        at = pl.multiple_of(c * (cols // 2) + n * piece, piece)
        return yall.at[k, pl.ds(at, piece), :]

    def background(k, n):
        return pltpu.make_async_remote_copy(
            span(0, n, core), span(k, n, core), bs.at[n, k], br.at[n, k],
            device_id={"grp": grp_peer(k)}, device_id_type=MESH)

    def hand(k, n):
        return pltpu.make_async_remote_copy(
            span(k, n, core), span(k, n, core), ks.at[n, k], kr.at[n, k],
            device_id={"dev": sib}, device_id_type=MESH)

    def quarter(k, n, h):
        at = pl.multiple_of(
            core * (cols // 2) + n * piece + h * (piece // 2), piece // 2)
        return yall.at[k, pl.ds(at, piece // 2), :]

    def passed(n, h):
        return pltpu.make_async_remote_copy(
            quarter(1 + h, n, h), quarter(3, n, h), bs.at[n, 4 + h], br.at[n, 4 + h],
            device_id={"grp": grp_peer(2 - h)}, device_id_type=MESH)

    def send_on(n):
        for k in range(1, 3 if relayed else G):
            background(k, n).start()
        if relayed:
            @pl.when(n == ITERS - 1)
            def _():
                background(3, n).start()

    def hand_on(n, last=False):
        for k in range(1, 3 if relayed else G):
            background(k, n).wait_recv()
            if relayed and not last:
                passed(n, k - 1).start()
            hand(k, n).start()

    def hand_diagonal(n):
        if relayed:
            for h in range(2):
                passed(n, h).wait_recv()
            hand(3, n).start()

    def sweep(n, carry):
        rd = log_rows - row_lse(n)
        send_on(n)

        @pl.when(n > 0)
        def _():
            hand_on(n - 1)

        @pl.when(n > 1)
        def _():
            hand_diagonal(n - 2)

        fs = [expand(rd[t:t + 1, :]) for t in range(tiles)]
        tops = [jnp.max(fs[t] - cost[t * TILE:(t + 1) * TILE, :], axis=0, keepdims=True)
                for t in range(tiles)]
        top = functools.reduce(jnp.maximum, tops)
        s = functools.reduce(lambda a, b: a + b, [
            jnp.sum(jnp.exp2(fs[t] - cost[t * TILE:(t + 1) * TILE, :] - top), axis=0, keepdims=True)
            for t in range(tiles)])
        low = top + jnp.log(s) * LOG2E
        for j in range(cols // TILE):
            colbuf[n, 0, j:j + 1, :] = low[:, j * TILE:(j + 1) * TILE]
        for k in range(1, V):
            pltpu.make_async_remote_copy(
                colbuf.at[n, 0], colbuf.at[n, k], cs.at[n], cr.at[n],
                device_id={"dev": dev_peer(k)}, device_id_type=MESH).start()
        others = colbuf.at[n, pl.ds(1, V - 1)]
        wait_all(others, cr.at[n])
        cd = log_cols - merge([colbuf[n, k] for k in range(V)])
        for j in range(cols // TILE):
            dual[0:1, j * TILE:(j + 1) * TILE] = cd[j:j + 1, :]
        return carry

    lax.fori_loop(0, ITERS, sweep, 0)
    shift = dual[0:1, :] - segsq[0:1, :] * unit
    for j in range(cols // TILE):
        gbuf[0, j:j + 1, :] = shift[:, j * TILE:(j + 1) * TILE]
    for k in range(1, G):
        pltpu.make_async_remote_copy(
            gbuf.at[0], gbuf.at[k], gs.at[0], gr.at[0],
            device_id={"grp": grp_peer(k)}, device_id_type=MESH).start()
    hand_on(ITERS - 1, True)
    hand_diagonal(ITERS - 2)
    if relayed:
        background(3, ITERS - 1).wait_recv()
        hand(3, ITERS - 1).start()

    first = pl.multiple_of(g * part, part)
    sq = jnp.zeros((part, 1), jnp.float32)
    for k in range(G):
        xf = xg[k, pl.ds(first, part), :].astype(jnp.float32)
        sq = sq + jnp.sum(xf * xf, axis=1, keepdims=True)
    for b in range(G):
        if b:
            for n in range(ITERS):
                hand(b, n).wait_recv()
        for k in range(G):
            at = pl.multiple_of((source(g, k, G) if k else g) * feats, feats)
            prod = lax.dot_general(
                xg[k, pl.ds(first, part), :], yall[b, :, pl.ds(at, feats)],
                (((1,), (1,)), ((), ())), preferred_element_type=jnp.float32)
            cross = prod if k == 0 else cross + prod
        cost[b * part:(b + 1) * part, :] = (sq - 2.0 * cross) * unit
    others = gbuf.at[pl.ds(1, G - 1)]
    wait_all(others, gs.at[0])
    wait_all(others, gr.at[0])
    tops = []
    for b in range(G):
        block = slice(b * part, (b + 1) * part)
        for j in range(cols // TILE):
            dual[0:1, j * TILE:(j + 1) * TILE] = gbuf[b, j:j + 1, :]
        logits = dual[0:1, :] - cost[block, :]
        cost[block, :] = logits
        tops.append(jnp.max(logits, axis=1, keepdims=True))
    top = functools.reduce(jnp.maximum, tops)
    s = functools.reduce(lambda a, b: a + b, [
        jnp.sum(jnp.exp2(cost[b * part:(b + 1) * part, :] - top), axis=1, keepdims=True)
        for b in range(G)])
    total = top + jnp.log(s) * LOG2E
    for b in range(G):
        wbuf[b] = jnp.exp2(cost[b * part:(b + 1) * part, :] - total).astype(jnp.bfloat16)

    def product(p):
        at = pl.multiple_of(p * feats, feats)
        acc = None
        for b in range(G):
            term = jnp.dot(wbuf[b], yall[b, :, pl.ds(at, feats)],
                           preferred_element_type=jnp.float32)
            acc = term if acc is None else acc + term
        return acc

    ocopies = {}
    for k in range(G - 1, 0, -1):
        sendbuf[k - 1] = product(grp_peer(k)).astype(jnp.bfloat16)
        ocopies[k] = pltpu.make_async_remote_copy(
            sendbuf.at[k - 1], recvbuf.at[k - 1], os.at[k], orr.at[k],
            device_id={"grp": grp_peer(k)}, device_id_type=MESH)
        ocopies[k].start()
    out_ref[pl.ds(first, part), :] = product(g)
    for k in range(1, G):
        ocopies[k].wait_recv()
        at = pl.multiple_of(source(g, k, G) * part, part)
        out_ref[pl.ds(at, part), :] = recvbuf[k - 1].astype(jnp.float32)
    for c in ocopies.values():
        c.wait_send()

    def drain(n, carry):
        wait_all(colbuf.at[n, pl.ds(1, V - 1)], cs.at[n])
        wait_all(rowbuf.at[n, pl.ds(1, G - 1)], rs.at[n])
        for k in range(1, G):
            if not (relayed and k == 3):
                background(k, n).wait_send()
            hand(k, n).wait_send()
        if relayed:
            @pl.when(n < ITERS - 1)
            def _():
                for h in range(2):
                    passed(n, h).wait_send()

            @pl.when(n == ITERS - 1)
            def _():
                background(3, n).wait_send()
        return carry

    lax.fori_loop(0, ITERS, drain, 0)
    for k in range(1, G):
        for h in range(2):
            noise(k, h).wait_send()
    own.wait_send()
    for s in range(C - 1):
        for h in range(CUTS):
            for way in (1, -1):
                @pl.when(ahead(-way, s + 1))
                def _():
                    hand_half(way, s, h).wait_send()

                @pl.when(jnp.logical_and(ahead(-way, s), ahead(way, 1)))
                def _():
                    hop(way, s, h).wait_send()


def solution(mesh):
    G, V = mesh.shape["grp"], mesh.shape["dev"]

    def local(x, y):
        rows, feats = x.shape
        segs, D = y.shape
        cols = segs * V
        dma = pltpu.SemaphoreType.DMA
        held = 2 * G * cols * D + 4 * rows * cols + 4 * G * rows * feats
        limit = min(held + held // 4 + 6 * 2**20, 60 * 2**20)
        f32, bf16 = jnp.float32, jnp.bfloat16
        return pl.pallas_call(
            functools.partial(kernel, G, V),
            out_shape=jax.ShapeDtypeStruct((rows, feats), f32),
            in_specs=[pl.BlockSpec(memory_space=pltpu.HBM)] * 2,
            out_specs=pl.BlockSpec(memory_space=pltpu.VMEM),
            scratch_shapes=[
                pltpu.VMEM((G, rows, feats), bf16),
                pltpu.VMEM((G, cols, D), bf16),
                pltpu.VMEM((rows, cols), f32),
                pltpu.VMEM((ITERS, G, rows // TILE, TILE), f32),
                pltpu.VMEM((ITERS, V, cols // TILE, TILE), f32),
                pltpu.VMEM((G, cols // TILE, TILE), f32),
                pltpu.VMEM((1, cols), f32),
                pltpu.VMEM((1, cols), f32),
                pltpu.VMEM((G, rows // G, cols), bf16),
                pltpu.VMEM((G - 1, rows // G, feats), bf16),
                pltpu.VMEM((G - 1, rows // G, feats), bf16),
                dma((G, 2)), dma((G, 2)),
                dma((2, V // 2 - 1, CUTS)), dma((2, V // 2 - 1, CUTS)),
                dma((2, V // 2 - 1, CUTS)), dma((2, V // 2 - 1, CUTS)),
                dma((ITERS,)), dma((ITERS,)),
                dma((ITERS,)), dma((ITERS,)),
                dma((G,)), dma((G,)),
                dma((2,)), dma((1,)), dma((1,)),
                dma((ITERS, G + 2)), dma((ITERS, G + 2)),
                dma((ITERS, G)), dma((ITERS, G)),
            ],
            compiler_params=pltpu.CompilerParams(
                collective_id=0, has_side_effects=True, vmem_limit_bytes=limit),
        )(x, y)

    placed = (P("dev", "grp"), P(("grp", "dev"), None))
    return jax.shard_map(
        local, mesh=mesh, in_specs=placed, out_specs=P("dev", "grp"), check_vma=False)
```
